32 devices in a mesh: groups: 2 (over x), expert: 8 (over z, y), dp: 2 (over core).
Axes of the slice: x: 2, y: 2, z: 4, core: 2. Of those that a mesh axis runs over, the one named last changes fastest.
Arguments:
- output_grad: bfloat16 [2048, 4096], P(('groups', 'expert', 'dp')), parts along dimension 0, may hold values from -6 to 6
- route_weights: float32 [2048, 2], P(('groups', 'expert', 'dp')), parts along dimension 0, may hold values from 0.2 to 1
- routes: int32 [2048, 2], P(('groups', 'expert', 'dp')), parts along dimension 0, may hold values from 0 to 7, as said below
- route_slots: int32 [2048, 2], P(('groups', 'expert', 'dp')), parts along dimension 0, may hold values from 0 to 11, as said below
- counts: int32 [32, 2], P(('groups', 'expert', 'dp')), parts along dimension 0, may hold values from 1 to 12, as said below
- saved_gate: bfloat16 [4, 96, 16384], P(('groups', 'dp'), None, 'expert'), parts along dimension 0, may hold values from -6 to 6
- saved_up: bfloat16 [4, 96, 16384], P(('groups', 'dp'), None, 'expert'), parts along dimension 0, may hold values from -6 to 6
- gate_weight: bfloat16 [4096, 16384], P(None, 'expert'), may hold values from -0.09375 to 0.09375
- up_weight: bfloat16 [4096, 16384], P(None, 'expert'), may hold values from -0.09375 to 0.09375
- down_weight: bfloat16 [16384, 4096], P('expert'), may hold values from -0.0625 to 0.0625
Outputs:
- token_grad: bfloat16 [2048, 4096], P(('groups', 'expert', 'dp')), parts along dimension 0
- down_grad: float32 [32768, 4096], P(('groups', 'expert', 'dp')), parts along dimension 0
The draws below stay inside these ranges and needn't reach their ends.
There are 2 independent parts, one for each index of `groups`. The reference program is written for one: setup_inputs(seed, part) draws one part's arguments, and reference() takes and returns one part's arrays. A program takes and returns all parts, laid end to end along the dimension named above; an argument that names none is the same for every part. Nothing has to cross between parts.
Inputs may be any that keep to these rules, and one draw needn't show every extreme that they name: `routes`: each token names two different experts; for each owner and each expert x below 2, exactly counts[owner, x] of the owner's tokens name x. `route_slots`: where a token names an expert x below 2, its slot is below counts[owner, x], and the owner's tokens that name x hold distinct slots. Row o counts the tokens of owner o that name each expert below 2.
All inputs are finite; a program needn't handle non-finite values.
Results may differ from the reference program's by a relative error of at most 0.0064.
Values may be sent and summed in bfloat16 or wider, within the bound.
A program may use at most 256 MiB of HBM per device.

```python
import jax
import jax.numpy as jnp
from jax import lax

D = 4096
EXPERTS = 8
FF_WIN = 8192
EXP_WIN = 2
TOK_DEV = 64
CAP = 12
SENDERS = 8
DATA = 2
OWNERS = 16
TOKENS = 1024
S_ROWS = 96
SHARDS = 4
FF_DEV = 2048


def routing_tables(key):
    keys = jax.random.split(key, 7)
    counts = jnp.minimum(jax.random.randint(keys[0], (OWNERS, EXP_WIN), 1, CAP + 3), CAP)
    pick = jax.random.randint(keys[1], (1, EXP_WIN), 0, OWNERS)
    owner_index = jnp.arange(OWNERS, dtype=jnp.int32)[:, None]
    counts = jnp.where(owner_index == pick, CAP, counts).astype(jnp.int32)
    scores = jax.random.randint(keys[2], (OWNERS, EXP_WIN, TOK_DEV), 0, 1 << 20) * TOK_DEV + jnp.arange(TOK_DEV, dtype=jnp.int32)
    order = jnp.argsort(scores, axis=-1)
    ranks = jnp.argsort(order, axis=-1).astype(jnp.int32)
    member = ranks < counts[:, :, None]
    in_first = member[:, 0]
    in_second = member[:, 1]
    others = EXPERTS - EXP_WIN
    first_other = EXP_WIN + jax.random.randint(keys[3], (OWNERS, TOK_DEV), 0, others)
    second_other = EXP_WIN + (first_other - EXP_WIN + jax.random.randint(keys[4], (OWNERS, TOK_DEV), 1, others)) % others
    column_a = jnp.where(in_first, 0, jnp.where(in_second, 1, first_other))
    column_b = jnp.where(in_first & in_second, 1, jnp.where(in_first | in_second, first_other, second_other))
    spare = jax.random.randint(keys[5], (OWNERS, TOK_DEV, 2), 0, CAP)
    slot_a = jnp.where(in_first, ranks[:, 0], jnp.where(in_second, ranks[:, 1], spare[:, :, 0]))
    slot_b = jnp.where(in_first & in_second, ranks[:, 1], spare[:, :, 1])
    swapped = jax.random.randint(keys[6], (OWNERS, TOK_DEV), 0, 2) == 1
    routes = jnp.stack([jnp.where(swapped, column_b, column_a), jnp.where(swapped, column_a, column_b)], -1)
    slots = jnp.stack([jnp.where(swapped, slot_b, slot_a), jnp.where(swapped, slot_a, slot_b)], -1)
    return (routes.reshape(OWNERS * TOK_DEV, 2).astype(jnp.int32), slots.reshape(OWNERS * TOK_DEV, 2).astype(jnp.int32), counts)


def draw_routes(key, part):
    return routing_tables(key)[0]


def draw_route_slots(key, part):
    return routing_tables(key)[1]


def draw_counts(key, part):
    return routing_tables(key)[2]


def steps_of(key, extent, shards, low, top_value):
    def one(position, blocks):
        heights = jax.random.uniform(jax.random.fold_in(jax.random.fold_in(key, 6), position), (blocks,), jnp.float32, low / len(shards), top_value / len(shards))
        return jnp.repeat(jnp.exp(heights), extent[position] // blocks).reshape((-1,) + (1,) * (len(extent) - position - 1))

    gain = one(*shards[0])
    for cut in shards[1:]:
        gain = gain * one(*cut)
    return gain


def bell_draw(key, dims, scale, reach, cuts=(), kind=jnp.bfloat16):
    factor_of = steps_of(key, dims, cuts, -0.22, 0.18) if cuts else 1.0
    values = jax.random.normal(key, dims, jnp.float32) * scale * factor_of
    return jnp.minimum(jnp.maximum(values, -reach), reach).astype(kind)


def setup_inputs(seed: int = 0, part: int = 0) -> dict:
    seeds = jax.random.split(jax.random.key(seed), 11)
    own_keys = jax.random.split(jax.random.fold_in(seeds[10], part), 11)
    return {
        "output_grad": bell_draw(own_keys[0], (TOKENS, D), 1.0, 6.0, ((0, 16),)),
        "route_weights": jnp.clip(0.2 + 0.8 * jax.random.uniform(own_keys[1], (TOKENS, 2), jnp.float32) ** steps_of(own_keys[1], (TOKENS, 2), ((0, 16),), -0.2, 0.2), 0.2, 1.0),
        "routes": draw_routes(jax.random.fold_in(jax.random.fold_in(seeds[10], part), 71), part),
        "route_slots": draw_route_slots(jax.random.fold_in(jax.random.fold_in(seeds[10], part), 71), part),
        "counts": draw_counts(jax.random.fold_in(jax.random.fold_in(seeds[10], part), 71), part),
        "saved_gate": bell_draw(own_keys[5], (DATA, S_ROWS, EXP_WIN * FF_WIN), 1.0, 6.0, ((0, 2), (2, 8))),
        "saved_up": bell_draw(own_keys[6], (DATA, S_ROWS, EXP_WIN * FF_WIN), 1.0, 6.0, ((0, 2), (2, 8))),
        "gate_weight": bell_draw(seeds[7], (D, EXP_WIN * FF_WIN), D ** -0.5, 0.09375, ((1, 8),)),
        "up_weight": bell_draw(seeds[8], (D, EXP_WIN * FF_WIN), D ** -0.5, 0.09375, ((1, 8),)),
        "down_weight": bell_draw(seeds[9], (EXP_WIN * FF_WIN, D), FF_WIN ** -0.5, 0.0625, ((0, 8),)),
    }


def route_table(routes, route_slots, counts, masked):
    experts = jnp.arange(EXP_WIN, dtype=jnp.int32)
    places = jnp.arange(CAP, dtype=jnp.int32)
    by_expert = routes.reshape(OWNERS, TOK_DEV, 2, 1, 1) == experts.reshape(1, 1, 1, EXP_WIN, 1)
    by_place = route_slots.reshape(OWNERS, TOK_DEV, 2, 1, 1) == places.reshape(1, 1, 1, 1, CAP)
    table = by_expert & by_place
    if masked:
        live = places.reshape(1, 1, CAP) < counts.reshape(OWNERS, EXP_WIN, 1)
        table = table & live[:, None, None, :, :]
    return table.astype(jnp.float32)


def reference(output_grad, route_weights, routes, route_slots, counts, saved_gate, saved_up, gate_weight, up_weight, down_weight):
    scaled = (route_weights[:, :, None] * output_grad[:, None, :].astype(jnp.float32)).astype(jnp.bfloat16)
    table = route_table(routes, route_slots, counts, True)
    packed = jnp.einsum("otkxc,otkd->oxcd", table, scaled.reshape(OWNERS, TOK_DEV, 2, D).astype(jnp.float32), precision=lax.Precision.HIGHEST).astype(jnp.bfloat16)
    expert_rows = packed.reshape(SENDERS, DATA, EXP_WIN, CAP, D).transpose(1, 2, 0, 3, 4).reshape(DATA, EXP_WIN, S_ROWS, D)
    returned_blocks = []
    grad_blocks = []
    for data_index in range(DATA):
        returned_blocks.append([])
    for expert in range(EXP_WIN):
        low = expert * FF_WIN
        gate_block = gate_weight[:, low:low + FF_WIN]
        up_block = up_weight[:, low:low + FF_WIN]
        down_block = down_weight[low:low + FF_WIN]
        grad_total = jnp.zeros((FF_WIN, D), jnp.float32)
        for data_index in range(DATA):
            rows = expert_rows[data_index, expert]
            gate_values = saved_gate[data_index, :, low:low + FF_WIN].astype(jnp.float32)
            up_values = saved_up[data_index, :, low:low + FF_WIN].astype(jnp.float32)
            upstream = jnp.dot(rows, down_block.T, preferred_element_type=jnp.float32)
            sigmoid_gate = jax.nn.sigmoid(gate_values)
            grad_up = (upstream * gate_values * sigmoid_gate).astype(jnp.bfloat16)
            grad_gate = (upstream * up_values * sigmoid_gate * (1.0 + gate_values * (1.0 - sigmoid_gate))).astype(jnp.bfloat16)
            hidden = (gate_values * sigmoid_gate * up_values).astype(jnp.bfloat16)

            def add_shard(shard, total):
                first = (shard * FF_DEV).astype(jnp.int32)
                part_gate = lax.dynamic_slice_in_dim(grad_gate, first, FF_DEV, 1)
                part_up = lax.dynamic_slice_in_dim(grad_up, first, FF_DEV, 1)
                weight_gate = lax.dynamic_slice_in_dim(gate_block, first, FF_DEV, 1)
                weight_up = lax.dynamic_slice_in_dim(up_block, first, FF_DEV, 1)
                term = jnp.dot(part_gate, weight_gate.T, preferred_element_type=jnp.float32) + jnp.dot(part_up, weight_up.T, preferred_element_type=jnp.float32)
                rounded = lax.optimization_barrier(term.astype(jnp.bfloat16))
                return total + rounded.astype(jnp.float32)

            summed = lax.fori_loop(jnp.int32(0), jnp.int32(SHARDS), add_shard, jnp.zeros((S_ROWS, D), jnp.float32))
            returned_blocks[data_index].append(summed)
            grad_total = grad_total + jnp.dot(hidden.T, rows, preferred_element_type=jnp.float32)
        grad_blocks.append(grad_total)
    returned = jnp.stack([jnp.stack(blocks, 0) for blocks in returned_blocks], 0)
    owner_returned = returned.reshape(DATA, EXP_WIN, SENDERS, CAP, D).transpose(2, 0, 1, 3, 4).reshape(OWNERS, EXP_WIN, CAP, D)
    pick = route_table(routes, route_slots, counts, False)
    token_grad = jnp.einsum("otkxc,oxcd->otd", pick, owner_returned, precision=lax.Precision.HIGHEST)
    token_grad = token_grad.reshape(TOKENS, D).astype(jnp.bfloat16)
    down_grad = jnp.concatenate(grad_blocks, 0)
    return token_grad, down_grad
```

```python
import functools

import jax
import jax.numpy as jnp
from jax import lax
from jax.experimental import pallas as pl
from jax.experimental.pallas import tpu as pltpu
from jax.sharding import PartitionSpec as P

EXP_WIN = 2
QUAD = 4
PAD = 16
CHUNKS = 4
MESH = pl.DeviceIdType.MESH
F32 = jnp.float32
BF16 = jnp.bfloat16
NT = (((1,), (1,)), ((), ()))
TN = (((0,), (0,)), ((), ()))


def pass_kernel(
    cap,
    og_ref,
    rw_ref,
    rt_ref,
    sl_ref,
    ct_ref,
    sgate_ref,
    sup_ref,
    gw_ref,
    uw_ref,
    dw_ref,
    tok_ref,
    hid_out,
    rows_out,
    gw,
    uw,
    dw,
    sg,
    su,
    rows,
    far_out,
    up,
    fac_g,
    fac_u,
    hid,
    part,
    core_out,
    core_in,
    summed,
    quad_in,
    far_ret,
    far_in,
    near_ret,
    w_sem,
    l_sem,
    o_sem,
    sv_send,
    sv_recv,
    fd_send,
    fd_recv,
    qd_send,
    qd_recv,
    cd_send,
    cd_recv,
    cr_send,
    cr_recv,
    qr_send,
    qr_recv,
    fr_send,
    fr_recv,
):
    g = lax.axis_index("groups")
    e = lax.axis_index("expert")
    d = lax.axis_index("dp")
    half = e // QUAD
    r = e % QUAD
    far = (1 - half) * QUAD + r
    core_peer = (g, e, 1 - d)
    far_peer = (g, far, d)

    def quad_rank(rel):
        hi, lo = r // 2, r % 2
        if rel & 2:
            hi = 1 - hi
        if rel & 1:
            lo = 1 - lo
        return hi * 2 + lo

    def quad_peer(rel):
        return (g, half * QUAD + quad_rank(rel), d)

    ff = dw.shape[0]
    width = dw.shape[1]
    step = width // CHUNKS
    group = rows.shape[0] // 2

    mine = pl.multiple_of(d * ff, ff)
    loads = [
        pltpu.make_async_copy(sgate_ref.at[0, :, pl.ds(mine, ff)], sg.at[d], l_sem.at[0]),
        pltpu.make_async_copy(sup_ref.at[0, :, pl.ds(mine, ff)], su.at[d], l_sem.at[1]),
    ]
    for c in loads:
        c.start()
    w_dw = [
        pltpu.make_async_copy(
            dw_ref.at[pl.ds(mine, ff), pl.ds(c * step, step)],
            dw.at[:, pl.ds(c * step, step)],
            w_sem.at[0, c],
        )
        for c in range(CHUNKS)
    ]
    w_gw = [
        pltpu.make_async_copy(
            gw_ref.at[pl.ds(c * step, step), pl.ds(mine, ff)],
            gw.at[pl.ds(c * step, step), :],
            w_sem.at[1, c],
        )
        for c in range(CHUNKS)
    ]
    w_uw = [
        pltpu.make_async_copy(
            uw_ref.at[pl.ds(c * step, step), pl.ds(mine, ff)],
            uw.at[pl.ds(c * step, step), :],
            w_sem.at[2, c],
        )
        for c in range(CHUNKS)
    ]
    for c in range(CHUNKS):
        w_dw[c].start()
    for c in range(CHUNKS):
        w_gw[c].start()
        w_uw[c].start()

    barrier = pltpu.get_barrier_semaphore()
    for peer in (core_peer, far_peer, quad_peer(1), quad_peer(2), quad_peer(3)):
        pl.semaphore_signal(barrier, inc=1, device_id=peer, device_id_type=MESH)
    pl.semaphore_wait(barrier, 5)

    def remote(src, dst, ss, rs, peer):
        return pltpu.make_async_remote_copy(
            src_ref=src, dst_ref=dst, send_sem=ss, recv_sem=rs, device_id=peer, device_id_type=MESH
        )

    theirs = pl.multiple_of((1 - d) * ff, ff)
    saved = [
        remote(
            sgate_ref.at[0, :, pl.ds(theirs, ff)], sg.at[d], sv_send.at[0], sv_recv.at[0], core_peer
        ),
        remote(
            sup_ref.at[0, :, pl.ds(theirs, ff)], su.at[d], sv_send.at[1], sv_recv.at[1], core_peer
        ),
    ]

    tokens = og_ref.shape[0]
    lane = lax.broadcasted_iota(jnp.int32, (tokens, EXP_WIN * PAD), 1)
    lane_x = lane // PAD
    lane_c = lane % PAD
    live_count = jnp.where(lane_x == 0, ct_ref[0:1, 0:1], ct_ref[0:1, 1:2])
    match = [
        (rt_ref[:, k : k + 1] == lane_x) & (sl_ref[:, k : k + 1] == lane_c) & (lane_c < cap)
        for k in range(2)
    ]
    placing = [
        jnp.where(m & (lane_c < live_count), 1.0, 0.0).astype(BF16) for m in match
    ]

    def slot(owner):
        return pl.multiple_of(d * group + ((owner % QUAD) * 2 + owner // QUAD) * PAD, PAD)

    own_at = slot(e)
    far_at = slot(far)
    far_send, quad_near, quad_far, core_send = [], [], [], []
    for c in range(CHUNKS):
        cols = pl.ds(c * step, step)
        og = og_ref[:, cols].astype(F32)
        packed = jnp.zeros((EXP_WIN * PAD, step), F32)
        for k in range(2):
            scaled = (rw_ref[:, k : k + 1] * og).astype(BF16)
            packed = packed + lax.dot_general(placing[k], scaled, TN, preferred_element_type=F32)
        first, second = packed[:PAD], packed[PAD:]
        rows[pl.ds(own_at, PAD), cols] = jnp.where(half == 0, first, second).astype(BF16)
        far_out[:, cols] = jnp.where(half == 0, second, first).astype(BF16)
        cp = remote(
            far_out.at[:, cols],
            rows.at[pl.ds(own_at, PAD), cols],
            fd_send.at[c],
            fd_recv.at[c],
            far_peer,
        )
        cp.start()
        far_send.append(cp)
        near = []
        for rel in (1, 2, 3):
            cp = remote(
                rows.at[pl.ds(own_at, PAD), cols],
                rows.at[pl.ds(own_at, PAD), cols],
                qd_send.at[0, rel - 1, c],
                qd_recv.at[0, rel - 1, c],
                quad_peer(rel),
            )
            cp.start()
            near.append(cp)
        quad_near.append(near)
    for cp in saved:
        cp.start()

    for cp in loads:
        cp.wait()
    for cp in saved:
        cp.wait_recv()
    samples = sg.shape[1]
    ri = lax.broadcasted_iota(jnp.int32, (group, samples), 0)
    ci = lax.broadcasted_iota(jnp.int32, (group, samples), 1)
    block = ri // PAD
    place = ri % PAD
    owner = (block % 2) * QUAD + block // 2
    spread = jnp.where((ci == owner * cap + place) & (place < cap), 1.0, 0.0).astype(BF16)
    piece = 256
    for dd in range(2):
        for q in range(ff // piece):
            cols = pl.ds(q * piece, piece)
            at = pl.ds(dd * group, group)
            gv = jnp.dot(spread, sg[dd, :, cols], preferred_element_type=F32)
            uv = jnp.dot(spread, su[dd, :, cols], preferred_element_type=F32)
            s = jax.nn.sigmoid(gv)
            gs = gv * s
            fac_u[at, cols] = gs
            fac_g[at, cols] = uv * s * (1.0 + gv * (1.0 - s))
            hid[at, cols] = (gs * uv).astype(BF16)
    out_hid = pltpu.make_async_copy(hid, hid_out, o_sem.at[0])
    out_hid.start()

    for c in range(CHUNKS):
        cols = pl.ds(c * step, step)
        far_send[c].wait_recv()
        copies = []
        for rel in (1, 2, 3):
            cp = remote(
                rows.at[pl.ds(far_at, PAD), cols],
                rows.at[pl.ds(far_at, PAD), cols],
                qd_send.at[1, rel - 1, c],
                qd_recv.at[1, rel - 1, c],
                quad_peer(rel),
            )
            cp.start()
            copies.append(cp)
        quad_far.append(copies)

    own_rows = pl.ds(pl.multiple_of(d * group, group), group)
    other_rows = pl.ds(pl.multiple_of((1 - d) * group, group), group)

    def upstream_chunk(c):
        cols = pl.ds(c * step, step)
        core_send[c].wait_recv()
        w_dw[c].wait()
        term = lax.dot_general(rows[:, cols], dw[:, cols], NT, preferred_element_type=F32)
        if c == 0:
            up[...] = term
        else:
            up[...] += term

    for c in range(CHUNKS):
        cols = pl.ds(c * step, step)
        for rel in (1, 2, 3):
            quad_near[c][rel - 1].wait_recv()
            quad_far[c][rel - 1].wait_recv()
        cp = remote(
            rows.at[own_rows, cols],
            rows.at[own_rows, cols],
            cd_send.at[c],
            cd_recv.at[c],
            core_peer,
        )
        cp.start()
        core_send.append(cp)
        if c > 0:
            upstream_chunk(c - 1)
    upstream_chunk(CHUNKS - 1)
    out_rows = pltpu.make_async_copy(rows, rows_out, o_sem.at[1])
    out_rows.start()

    gg = (up[...] * fac_g[...]).astype(BF16)
    gu = (up[...] * fac_u[...]).astype(BF16)

    core_ret, quad_ret, far_back = [], [], []

    def stage_a(c):
        w_gw[c].wait()
        w_uw[c].wait()
        at = pl.ds(c * step, step)
        part[c] = lax.dot_general(gg, gw[at, :], NT, preferred_element_type=F32) + lax.dot_general(
            gu, uw[at, :], NT, preferred_element_type=F32
        )
        core_out[c] = part[c, other_rows, :].astype(BF16)
        cp = remote(core_out.at[c], core_in.at[c], cr_send.at[c], cr_recv.at[c], core_peer)
        cp.start()
        core_ret.append(cp)

    def stage_b(c):
        core_ret[c].wait_recv()
        summed[c] = (part[c, own_rows, :] + core_in[c].astype(F32)).astype(BF16)
        copies = []
        for rel in (1, 2, 3):
            at = pl.multiple_of(quad_rank(rel) * 2 * PAD, 2 * PAD)
            cp = remote(
                summed.at[c, pl.ds(at, 2 * PAD), :],
                quad_in.at[rel - 1, c],
                qr_send.at[rel - 1, c],
                qr_recv.at[rel - 1, c],
                quad_peer(rel),
            )
            cp.start()
            copies.append(cp)
        quad_ret.append(copies)

    def stage_c(c):
        for cp in quad_ret[c]:
            cp.wait_recv()
        at = pl.multiple_of(r * 2 * PAD, 2 * PAD)
        total = summed[c, pl.ds(at, 2 * PAD), :].astype(F32)
        for rel in (1, 2, 3):
            total = total + quad_in[rel - 1, c].astype(F32)
        first, second = total[:PAD], total[PAD:]
        near_ret[c] = jnp.where(half == 0, first, second)
        far_ret[c] = jnp.where(half == 0, second, first).astype(BF16)
        cp = remote(far_ret.at[c], far_in.at[c], fr_send.at[c], fr_recv.at[c], far_peer)
        cp.start()
        far_back.append(cp)

    table = jnp.where(match[0], 1.0, 0.0) + jnp.where(match[1], 1.0, 0.0)
    table_near = jnp.where(half == 0, table[:, :PAD], table[:, PAD:]).astype(BF16)
    table_far = jnp.where(half == 0, table[:, PAD:], table[:, :PAD]).astype(BF16)

    def stage_d(c):
        far_back[c].wait_recv()
        near = near_ret[c]
        high = near.astype(BF16)
        low = (near - high.astype(F32)).astype(BF16)
        total = jnp.dot(table_near, high, preferred_element_type=F32)
        total = total + jnp.dot(table_near, low, preferred_element_type=F32)
        total = total + jnp.dot(table_far, far_in[c], preferred_element_type=F32)
        tok_ref[:, pl.ds(c * step, step)] = total.astype(BF16)

    for c in range(CHUNKS + 3):
        if c < CHUNKS:
            stage_a(c)
        if 0 <= c - 1 < CHUNKS:
            stage_b(c - 1)
        if 0 <= c - 2 < CHUNKS:
            stage_c(c - 2)
        if 0 <= c - 3 < CHUNKS:
            stage_d(c - 3)

    out_hid.wait()
    out_rows.wait()
    for cp in saved + far_send + core_send + core_ret + far_back:
        cp.wait_send()
    for group_of in quad_near + quad_far + quad_ret:
        for cp in group_of:
            cp.wait_send()


def local_fast(og, rw, rt, sl, ct, sgate, sup, gw, uw, dw):
    tokens, width = og.shape
    ff = dw.shape[0] // 2
    samples = sgate.shape[1]
    owners = lax.axis_size("expert")
    cap = samples // owners
    group = owners * PAD
    step = width // CHUNKS
    vmem = pl.BlockSpec(memory_space=pltpu.VMEM)
    hbm = pl.BlockSpec(memory_space=pl.ANY)
    dma = pltpu.SemaphoreType.DMA
    tok, hid, rows = pl.pallas_call(
        functools.partial(pass_kernel, cap),
        out_shape=(
            jax.ShapeDtypeStruct((tokens, width), BF16),
            jax.ShapeDtypeStruct((2 * group, ff), BF16),
            jax.ShapeDtypeStruct((2 * group, width), BF16),
        ),
        in_specs=[vmem] * 5 + [hbm] * 5,
        out_specs=(vmem, hbm, hbm),
        scratch_shapes=[
            pltpu.VMEM((width, ff), BF16),
            pltpu.VMEM((width, ff), BF16),
            pltpu.VMEM((ff, width), BF16),
            pltpu.VMEM((2, samples, ff), BF16),
            pltpu.VMEM((2, samples, ff), BF16),
            pltpu.VMEM((2 * group, width), BF16),
            pltpu.VMEM((PAD, width), BF16),
            pltpu.VMEM((2 * group, ff), F32),
            pltpu.VMEM((2 * group, ff), F32),
            pltpu.VMEM((2 * group, ff), F32),
            pltpu.VMEM((2 * group, ff), BF16),
            pltpu.VMEM((CHUNKS, 2 * group, step), F32),
            pltpu.VMEM((CHUNKS, group, step), BF16),
            pltpu.VMEM((CHUNKS, group, step), BF16),
            pltpu.VMEM((CHUNKS, group, step), BF16),
            pltpu.VMEM((3, CHUNKS, 2 * PAD, step), BF16),
            pltpu.VMEM((CHUNKS, PAD, step), BF16),
            pltpu.VMEM((CHUNKS, PAD, step), BF16),
            pltpu.VMEM((CHUNKS, PAD, step), F32),
            dma((3, CHUNKS)),
            dma((2,)),
            dma((2,)),
            dma((2,)),
            dma((2,)),
            dma((CHUNKS,)),
            dma((CHUNKS,)),
            dma((2, 3, CHUNKS)),
            dma((2, 3, CHUNKS)),
            dma((CHUNKS,)),
            dma((CHUNKS,)),
            dma((CHUNKS,)),
            dma((CHUNKS,)),
            dma((3, CHUNKS)),
            dma((3, CHUNKS)),
            dma((CHUNKS,)),
            dma((CHUNKS,)),
        ],
        compiler_params=pltpu.CompilerParams(
            collective_id=0, has_side_effects=True, vmem_limit_bytes=52 * 1024 * 1024
        ),
        cost_estimate=pl.CostEstimate(
            flops=12 * group * ff * width, bytes_accessed=6 * ff * width, transcendentals=2 * group * ff
        ),
    )(og, rw, rt, sl, ct, sgate, sup, gw, uw, dw)
    down = lax.dot_general(hid, rows, TN, preferred_element_type=F32)
    return tok, down


def local_plain(og, rw, rt, sl, ct, sgate, sup, gw, uw, dw):
    senders = lax.axis_size("expert")
    shards = senders // EXP_WIN
    capacity = sgate.shape[1] // senders
    tokens, width = og.shape
    places = jnp.arange(capacity, dtype=jnp.int32)
    experts = jnp.arange(EXP_WIN, dtype=jnp.int32)
    matches = (rt[:, :, None, None] == experts[None, None, :, None]) & (
        sl[:, :, None, None] == places[None, None, None, :]
    )
    live = places[None, :] < ct[0][:, None]
    scaled = (rw[:, :, None] * og[:, None, :].astype(F32)).astype(BF16)
    placing = (matches & live[None, None, :, :]).astype(BF16)
    packed = jnp.einsum("tkxc,tkd->xcd", placing, scaled, preferred_element_type=F32).astype(BF16)
    outgoing = jnp.repeat(packed, shards, axis=0)
    arrived = lax.all_to_all(outgoing, "expert", split_axis=0, concat_axis=0, tiled=True)
    rows = arrived.reshape(senders * capacity, width)
    gv = sgate[0].astype(F32)
    uv = sup[0].astype(F32)
    upstream = lax.dot_general(rows, dw, NT, preferred_element_type=F32)
    s = jax.nn.sigmoid(gv)
    grad_up = (upstream * gv * s).astype(BF16)
    grad_gate = (upstream * uv * s * (1.0 + gv * (1.0 - s))).astype(BF16)
    hidden = (gv * s * uv).astype(BF16)
    part = lax.dot_general(grad_gate, gw, NT, preferred_element_type=F32)
    part = part + lax.dot_general(grad_up, uw, NT, preferred_element_type=F32)
    table = jnp.sum(matches.astype(F32), axis=1).reshape(tokens, EXP_WIN * capacity)
    received = lax.all_to_all(
        part.astype(BF16).reshape(senders, capacity, width),
        "expert",
        split_axis=0,
        concat_axis=0,
        tiled=True,
    )
    summed = jnp.sum(received.reshape(EXP_WIN, shards, capacity, width), axis=1, dtype=F32)
    gathered = jnp.dot(
        table,
        summed.reshape(EXP_WIN * capacity, width),
        precision=lax.Precision.HIGHEST,
        preferred_element_type=F32,
    )
    both_hidden = lax.all_to_all(hidden, "dp", split_axis=1, concat_axis=0, tiled=True)
    both_rows = lax.all_gather(rows, "dp", axis=0, tiled=True)
    down = lax.dot_general(both_hidden, both_rows, TN, preferred_element_type=F32)
    return gathered.astype(BF16), down


def solution(mesh):
    tokens = P(("groups", "expert", "dp"), None)
    saved = P(("groups", "dp"), None, "expert")
    columns = P(None, "expert")
    fits = mesh.shape["expert"] == EXP_WIN * QUAD and mesh.shape["dp"] == 2
    return jax.shard_map(
        local_fast if fits else local_plain,
        mesh=mesh,
        in_specs=(tokens,) * 5 + (saved, saved, columns, columns, P("expert", None)),
        out_specs=(tokens, tokens),
        check_vma=False,
    )
```

```python
import functools

import jax
import jax.numpy as jnp
from jax import lax
from jax.experimental import pallas as pl
from jax.experimental.pallas import tpu as pltpu
from jax.sharding import PartitionSpec as P

EXP_WIN = 2
QUAD = 4
PAD = 16
CHUNKS = 2
DOWN_STEPS = 4
RELAY = (2, 1)
RELAY_BACK = (1, 2)
MESH = pl.DeviceIdType.MESH
F32 = jnp.float32
BF16 = jnp.bfloat16
NT = (((1,), (1,)), ((), ()))
TN = (((0,), (0,)), ((), ()))


def pass_kernel(
    cap,
    og_hbm,
    rw_hbm,
    rt_hbm,
    sl_hbm,
    ct_hbm,
    sgate_ref,
    sup_ref,
    gw_ref,
    uw_ref,
    dw_ref,
    tok_ref,
    hid_out,
    rows_out,
    og_ref,
    rw_ref,
    rt_ref,
    sl_ref,
    ct_ref,
    in_sem,
    gw,
    uw,
    dw,
    sg,
    su,
    rows,
    far_out,
    up,
    fac_g,
    fac_u,
    hid,
    part,
    core_out,
    core_in,
    summed,
    quad_in,
    relayed,
    far_ret,
    far_in,
    near_ret,
    w_sem,
    l_sem,
    o_sem,
    sv_send,
    sv_recv,
    fd_send,
    fd_recv,
    qd_send,
    qd_recv,
    cd_send,
    cd_recv,
    cr_send,
    cr_recv,
    qr_send,
    qr_recv,
    fr_send,
    fr_recv,
):
    g = lax.axis_index("groups")
    e = lax.axis_index("expert")
    d = lax.axis_index("dp")
    half = e // QUAD
    r = e % QUAD
    far = (1 - half) * QUAD + r
    core_peer = (g, e, 1 - d)
    far_peer = (g, far, d)

    def quad_rank(rel):
        hi, lo = r // 2, r % 2
        if rel & 2:
            hi = 1 - hi
        if rel & 1:
            lo = 1 - lo
        return hi * 2 + lo

    def quad_peer(rel):
        return (g, half * QUAD + quad_rank(rel), d)

    ff = dw.shape[0]
    width = dw.shape[1]
    step = width // CHUNKS
    group = rows.shape[0] // 2

    small = [
        pltpu.make_async_copy(src, dst, in_sem.at[i])
        for i, (src, dst) in enumerate(
            (
                (rt_hbm, rt_ref),
                (sl_hbm, sl_ref),
                (ct_hbm, ct_ref),
                (rw_hbm, rw_ref),
                (og_hbm, og_ref),
            )
        )
    ]
    for c in small:
        c.start()
    mine = pl.multiple_of(d * ff, ff)
    loads = [
        pltpu.make_async_copy(sgate_ref.at[0, :, pl.ds(mine, ff)], sg.at[d], l_sem.at[0]),
        pltpu.make_async_copy(sup_ref.at[0, :, pl.ds(mine, ff)], su.at[d], l_sem.at[1]),
    ]
    for c in loads:
        c.start()
    w_dw = [
        pltpu.make_async_copy(
            dw_ref.at[pl.ds(mine, ff), pl.ds(c * step, step)],
            dw.at[:, pl.ds(c * step, step)],
            w_sem.at[0, c],
        )
        for c in range(CHUNKS)
    ]
    w_gw = [
        pltpu.make_async_copy(
            gw_ref.at[pl.ds(c * step, step), pl.ds(mine, ff)],
            gw.at[pl.ds(c * step, step), :],
            w_sem.at[1, c],
        )
        for c in range(CHUNKS)
    ]
    w_uw = [
        pltpu.make_async_copy(
            uw_ref.at[pl.ds(c * step, step), pl.ds(mine, ff)],
            uw.at[pl.ds(c * step, step), :],
            w_sem.at[2, c],
        )
        for c in range(CHUNKS)
    ]
    barrier = pltpu.get_barrier_semaphore()
    for peer in (core_peer, far_peer, quad_peer(1), quad_peer(2)):
        pl.semaphore_signal(barrier, inc=1, device_id=peer, device_id_type=MESH)
    pl.semaphore_wait(barrier, 4)

    def remote(src, dst, ss, rs, peer):
        return pltpu.make_async_remote_copy(
            src_ref=src, dst_ref=dst, send_sem=ss, recv_sem=rs, device_id=peer, device_id_type=MESH
        )

    theirs = pl.multiple_of((1 - d) * ff, ff)
    saved = [
        remote(
            sgate_ref.at[0, :, pl.ds(theirs, ff)], sg.at[d], sv_send.at[0], sv_recv.at[0], core_peer
        ),
        remote(
            sup_ref.at[0, :, pl.ds(theirs, ff)], su.at[d], sv_send.at[1], sv_recv.at[1], core_peer
        ),
    ]

    for c in small:
        c.wait()
    tokens = og_ref.shape[0]
    line = lax.broadcasted_iota(jnp.int32, (EXP_WIN * PAD, tokens), 0)
    line_x = line // PAD
    line_c = line % PAD
    live_count = jnp.where(line_x == 0, ct_ref[0:1, 0:1], ct_ref[0:1, 1:2])
    match = [
        (rt_ref[k : k + 1, :] == line_x) & (sl_ref[k : k + 1, :] == line_c) & (line_c < cap)
        for k in range(2)
    ]
    placing = [
        jnp.where(m & (line_c < live_count), 1.0, 0.0).astype(BF16) for m in match
    ]
    same = lax.broadcasted_iota(jnp.int32, (tokens, tokens), 0) == lax.broadcasted_iota(
        jnp.int32, (tokens, tokens), 1
    )
    weight = [
        jnp.sum(jnp.where(same, rw_ref[k : k + 1, :], 0.0), axis=1, keepdims=True)
        for k in range(2)
    ]

    def slot(owner):
        return pl.multiple_of(d * group + ((owner % QUAD) * 2 + owner // QUAD) * PAD, PAD)

    def quad_copy(at, kind, source, c, rel):
        place = rows.at[pl.ds(at, PAD), pl.ds(c * step, step)]
        cp = remote(
            place, place, qd_send.at[kind, source, c], qd_recv.at[kind, source, c], quad_peer(rel)
        )
        cp.start()
        return cp

    own_at = slot(e)
    far_at = slot(far)
    far_send, quad_near, quad_far, core_send = [], [], [], []
    relay_near, relay_far = [], []
    for c in range(CHUNKS):
        cols = pl.ds(c * step, step)
        og = og_ref[:, cols].astype(F32)
        packed = jnp.zeros((EXP_WIN * PAD, step), F32)
        for k in range(2):
            scaled = (weight[k] * og).astype(BF16)
            packed = packed + jnp.dot(placing[k], scaled, preferred_element_type=F32)
        first, second = packed[:PAD], packed[PAD:]
        rows[pl.ds(own_at, PAD), cols] = jnp.where(half == 0, first, second).astype(BF16)
        far_out[:, cols] = jnp.where(half == 0, second, first).astype(BF16)
        cp = remote(
            far_out.at[:, cols],
            rows.at[pl.ds(own_at, PAD), cols],
            fd_send.at[c],
            fd_recv.at[c],
            far_peer,
        )
        cp.start()
        far_send.append(cp)
        quad_near.append([quad_copy(own_at, 0, rel - 1, c, rel) for rel in (1, 2)])
    for cp in saved:
        cp.start()
    for c in range(CHUNKS):
        w_dw[c].start()

    for cp in loads:
        cp.wait()
    for cp in saved:
        cp.wait_recv()
    samples = sg.shape[1]
    ri = lax.broadcasted_iota(jnp.int32, (group, samples), 0)
    ci = lax.broadcasted_iota(jnp.int32, (group, samples), 1)
    block = ri // PAD
    place = ri % PAD
    owner = (block % 2) * QUAD + block // 2
    spread = jnp.where((ci == owner * cap + place) & (place < cap), 1.0, 0.0).astype(BF16)
    piece = 256

    def relay(c, sent, kind):
        via = RELAY[c]
        sent[c][via - 1].wait_recv()
        source = (half if kind == 0 else 1 - half) * QUAD + quad_rank(via)
        return quad_copy(slot(source), kind, 2, c, 3 - via)

    for dd in range(2):
        for q in range(ff // piece):
            cols = pl.ds(q * piece, piece)
            at = pl.ds(dd * group, group)
            gv = jnp.dot(spread, sg[dd, :, cols], preferred_element_type=F32)
            uv = jnp.dot(spread, su[dd, :, cols], preferred_element_type=F32)
            s = jax.nn.sigmoid(gv)
            gs = gv * s
            fac_u[at, cols] = gs
            fac_g[at, cols] = uv * s * (1.0 + gv * (1.0 - s))
            hid[cols, at] = jnp.transpose(gs * uv).astype(BF16)
            if dd == 1 and q < CHUNKS:
                relay_near.append(relay(q, quad_near, 0))
    out_hid = pltpu.make_async_copy(hid, hid_out, o_sem.at[0])
    out_hid.start()

    own_rows = pl.ds(pl.multiple_of(d * group, group), group)
    other_rows = pl.ds(pl.multiple_of((1 - d) * group, group), group)

    def upstream_chunk(c):
        cols = pl.ds(c * step, step)
        core_send[c].wait_recv()
        w_dw[c].wait()
        term = lax.dot_general(rows[:, cols], dw[:, cols], NT, preferred_element_type=F32)
        if c == 0:
            up[...] = term
        else:
            up[...] += term

    for t in range(CHUNKS + 3):
        if t < CHUNKS:
            far_send[t].wait_recv()
            quad_far.append([quad_copy(far_at, 1, rel - 1, t, rel) for rel in (1, 2)])
            w_gw[t].start()
            w_uw[t].start()
        if 0 <= t - 1 < CHUNKS:
            relay_far.append(relay(t - 1, quad_far, 1))
        if 0 <= t - 2 < CHUNKS:
            c = t - 2
            cols = pl.ds(c * step, step)
            straight = 2 - RELAY[c]
            quad_near[c][straight].wait_recv()
            quad_far[c][straight].wait_recv()
            relay_near[c].wait_recv()
            relay_far[c].wait_recv()
            cp = remote(
                rows.at[own_rows, cols],
                rows.at[own_rows, cols],
                cd_send.at[c],
                cd_recv.at[c],
                core_peer,
            )
            cp.start()
            core_send.append(cp)
        if t >= 3:
            upstream_chunk(t - 3)
    out_rows = pltpu.make_async_copy(rows, rows_out, o_sem.at[1])
    out_rows.start()

    gg = (up[...] * fac_g[...]).astype(BF16)
    gu = (up[...] * fac_u[...]).astype(BF16)

    core_ret, quad_ret, far_back = [], [], []

    def stage_a(c):
        w_gw[c].wait()
        w_uw[c].wait()
        at = pl.ds(c * step, step)
        part[c] = lax.dot_general(gg, gw[at, :], NT, preferred_element_type=F32) + lax.dot_general(
            gu, uw[at, :], NT, preferred_element_type=F32
        )
        core_out[c] = part[c, other_rows, :].astype(BF16)
        cp = remote(core_out.at[c], core_in.at[c], cr_send.at[c], cr_recv.at[c], core_peer)
        cp.start()
        core_ret.append(cp)

    def stage_b(c):
        core_ret[c].wait_recv()
        summed[c] = (part[c, own_rows, :] + core_in[c].astype(F32)).astype(BF16)
        via = RELAY_BACK[c]
        copies = []
        for i, rank in enumerate((quad_rank(via), quad_rank(3))):
            cp = remote(
                summed.at[c, pl.ds(pl.multiple_of(rank * 2 * PAD, 2 * PAD), 2 * PAD), :],
                quad_in.at[i, c],
                qr_send.at[i, c],
                qr_recv.at[i, c],
                quad_peer(via),
            )
            cp.start()
            copies.append(cp)
        quad_ret.append(copies)

    def stage_r(c):
        rel = 3 - RELAY_BACK[c]
        quad_ret[c][1].wait_recv()
        at = pl.multiple_of(quad_rank(rel) * 2 * PAD, 2 * PAD)
        relayed[c] = (
            summed[c, pl.ds(at, 2 * PAD), :].astype(F32) + quad_in[1, c].astype(F32)
        ).astype(BF16)
        cp = remote(
            relayed.at[c], quad_in.at[2, c], qr_send.at[2, c], qr_recv.at[2, c], quad_peer(rel)
        )
        cp.start()
        quad_ret[c].append(cp)

    def stage_c(c):
        quad_ret[c][0].wait_recv()
        quad_ret[c][2].wait_recv()
        at = pl.multiple_of(r * 2 * PAD, 2 * PAD)
        total = summed[c, pl.ds(at, 2 * PAD), :].astype(F32)
        total = total + quad_in[0, c].astype(F32) + quad_in[2, c].astype(F32)
        first, second = total[:PAD], total[PAD:]
        near_ret[c] = jnp.where(half == 0, first, second)
        far_ret[c] = jnp.where(half == 0, second, first).astype(BF16)
        cp = remote(far_ret.at[c], far_in.at[c], fr_send.at[c], fr_recv.at[c], far_peer)
        cp.start()
        far_back.append(cp)

    table = jnp.where(match[0], 1.0, 0.0) + jnp.where(match[1], 1.0, 0.0)
    table_near = jnp.where(half == 0, table[:PAD], table[PAD:]).astype(BF16)
    table_far = jnp.where(half == 0, table[PAD:], table[:PAD]).astype(BF16)

    def stage_d(c):
        far_back[c].wait_recv()
        near = near_ret[c]
        high = near.astype(BF16)
        low = (near - high.astype(F32)).astype(BF16)
        total = lax.dot_general(table_near, high, TN, preferred_element_type=F32)
        total = total + lax.dot_general(table_near, low, TN, preferred_element_type=F32)
        total = total + lax.dot_general(table_far, far_in[c], TN, preferred_element_type=F32)
        tok_ref[:, pl.ds(c * step, step)] = total.astype(BF16)

    for t in range(CHUNKS + 4):
        for lag, stage in enumerate((stage_a, stage_b, stage_r, stage_c, stage_d)):
            if 0 <= t - lag < CHUNKS:
                stage(t - lag)

    out_hid.wait()
    out_rows.wait()
    for cp in saved + far_send + relay_near + relay_far + core_send + core_ret + far_back:
        cp.wait_send()
    for group_of in quad_near + quad_far + quad_ret:
        for cp in group_of:
            cp.wait_send()


def down_kernel(hid_ref, rows_ref, out_ref):
    out_ref[...] = jnp.dot(hid_ref[...], rows_ref[...], preferred_element_type=F32)


def local_fast(og, rw, rt, sl, ct, sgate, sup, gw, uw, dw):
    tokens, width = og.shape
    ff = dw.shape[0] // 2
    samples = sgate.shape[1]
    owners = lax.axis_size("expert")
    cap = samples // owners
    group = owners * PAD
    step = width // CHUNKS
    vmem = pl.BlockSpec(memory_space=pltpu.VMEM)
    hbm = pl.BlockSpec(memory_space=pl.ANY)
    dma = pltpu.SemaphoreType.DMA
    tok, hid, rows = pl.pallas_call(
        functools.partial(pass_kernel, cap),
        out_shape=(
            jax.ShapeDtypeStruct((tokens, width), BF16),
            jax.ShapeDtypeStruct((ff, 2 * group), BF16),
            jax.ShapeDtypeStruct((2 * group, width), BF16),
        ),
        in_specs=[hbm] * 10,
        out_specs=(vmem, hbm, hbm),
        scratch_shapes=[
            pltpu.VMEM(og.shape, BF16),
            pltpu.VMEM((2, tokens), F32),
            pltpu.VMEM((2, tokens), jnp.int32),
            pltpu.VMEM((2, tokens), jnp.int32),
            pltpu.VMEM(ct.shape, jnp.int32),
            dma((5,)),
            pltpu.VMEM((width, ff), BF16),
            pltpu.VMEM((width, ff), BF16),
            pltpu.VMEM((ff, width), BF16),
            pltpu.VMEM((2, samples, ff), BF16),
            pltpu.VMEM((2, samples, ff), BF16),
            pltpu.VMEM((2 * group, width), BF16),
            pltpu.VMEM((PAD, width), BF16),
            pltpu.VMEM((2 * group, ff), F32),
            pltpu.VMEM((2 * group, ff), F32),
            pltpu.VMEM((2 * group, ff), F32),
            pltpu.VMEM((ff, 2 * group), BF16),
            pltpu.VMEM((CHUNKS, 2 * group, step), F32),
            pltpu.VMEM((CHUNKS, group, step), BF16),
            pltpu.VMEM((CHUNKS, group, step), BF16),
            pltpu.VMEM((CHUNKS, group, step), BF16),
            pltpu.VMEM((3, CHUNKS, 2 * PAD, step), BF16),
            pltpu.VMEM((CHUNKS, 2 * PAD, step), BF16),
            pltpu.VMEM((CHUNKS, PAD, step), BF16),
            pltpu.VMEM((CHUNKS, PAD, step), BF16),
            pltpu.VMEM((CHUNKS, PAD, step), F32),
            dma((3, CHUNKS)),
            dma((2,)),
            dma((2,)),
            dma((2,)),
            dma((2,)),
            dma((CHUNKS,)),
            dma((CHUNKS,)),
            dma((2, 3, CHUNKS)),
            dma((2, 3, CHUNKS)),
            dma((CHUNKS,)),
            dma((CHUNKS,)),
            dma((CHUNKS,)),
            dma((CHUNKS,)),
            dma((3, CHUNKS)),
            dma((3, CHUNKS)),
            dma((CHUNKS,)),
            dma((CHUNKS,)),
        ],
        compiler_params=pltpu.CompilerParams(
            collective_id=0, has_side_effects=True, vmem_limit_bytes=60 * 1024 * 1024
        ),
        cost_estimate=pl.CostEstimate(
            flops=12 * group * ff * width, bytes_accessed=6 * ff * width, transcendentals=2 * group * ff
        ),
    )(og, rw.T, rt.T, sl.T, ct, sgate, sup, gw, uw, dw)
    tile = width // DOWN_STEPS
    down = pl.pallas_call(
        down_kernel,
        grid=(DOWN_STEPS,),
        in_specs=[
            pl.BlockSpec((ff, 2 * group), lambda i: (0, 0)),
            pl.BlockSpec((2 * group, tile), lambda i: (0, i)),
        ],
        out_specs=pl.BlockSpec((ff, tile), lambda i: (0, i)),
        out_shape=jax.ShapeDtypeStruct((ff, width), F32),
        compiler_params=pltpu.CompilerParams(vmem_limit_bytes=62 * 1024 * 1024),
        cost_estimate=pl.CostEstimate(
            flops=4 * group * ff * width, bytes_accessed=4 * ff * width, transcendentals=0
        ),
    )(hid, rows)
    return tok, down


def local_plain(og, rw, rt, sl, ct, sgate, sup, gw, uw, dw):
    senders = lax.axis_size("expert")
    shards = senders // EXP_WIN
    capacity = sgate.shape[1] // senders
    tokens, width = og.shape
    places = jnp.arange(capacity, dtype=jnp.int32)
    experts = jnp.arange(EXP_WIN, dtype=jnp.int32)
    matches = (rt[:, :, None, None] == experts[None, None, :, None]) & (
        sl[:, :, None, None] == places[None, None, None, :]
    )
    live = places[None, :] < ct[0][:, None]
    scaled = (rw[:, :, None] * og[:, None, :].astype(F32)).astype(BF16)
    placing = (matches & live[None, None, :, :]).astype(BF16)
    packed = jnp.einsum("tkxc,tkd->xcd", placing, scaled, preferred_element_type=F32).astype(BF16)
    outgoing = jnp.repeat(packed, shards, axis=0)
    arrived = lax.all_to_all(outgoing, "expert", split_axis=0, concat_axis=0, tiled=True)
    rows = arrived.reshape(senders * capacity, width)
    gv = sgate[0].astype(F32)
    uv = sup[0].astype(F32)
    upstream = lax.dot_general(rows, dw, NT, preferred_element_type=F32)
    s = jax.nn.sigmoid(gv)
    grad_up = (upstream * gv * s).astype(BF16)
    grad_gate = (upstream * uv * s * (1.0 + gv * (1.0 - s))).astype(BF16)
    hidden = (gv * s * uv).astype(BF16)
    part = lax.dot_general(grad_gate, gw, NT, preferred_element_type=F32)
    part = part + lax.dot_general(grad_up, uw, NT, preferred_element_type=F32)
    table = jnp.sum(matches.astype(F32), axis=1).reshape(tokens, EXP_WIN * capacity)
    received = lax.all_to_all(
        part.astype(BF16).reshape(senders, capacity, width),
        "expert",
        split_axis=0,
        concat_axis=0,
        tiled=True,
    )
    summed = jnp.sum(received.reshape(EXP_WIN, shards, capacity, width), axis=1, dtype=F32)
    gathered = jnp.dot(
        table,
        summed.reshape(EXP_WIN * capacity, width),
        precision=lax.Precision.HIGHEST,
        preferred_element_type=F32,
    )
    both_hidden = lax.all_to_all(hidden, "dp", split_axis=1, concat_axis=0, tiled=True)
    both_rows = lax.all_gather(rows, "dp", axis=0, tiled=True)
    down = lax.dot_general(both_hidden, both_rows, TN, preferred_element_type=F32)
    return gathered.astype(BF16), down


def solution(mesh):
    tokens = P(("groups", "expert", "dp"), None)
    saved = P(("groups", "dp"), None, "expert")
    columns = P(None, "expert")
    fits = mesh.shape["expert"] == EXP_WIN * QUAD and mesh.shape["dp"] == 2
    return jax.shard_map(
        local_fast if fits else local_plain,
        mesh=mesh,
        in_specs=(tokens,) * 5 + (saved, saved, columns, columns, P("expert", None)),
        out_specs=(tokens, tokens),
        check_vma=False,
    )
```

```python
import functools

import jax
import jax.numpy as jnp
from jax import lax
from jax.experimental import pallas as pl
from jax.experimental.pallas import tpu as pltpu
from jax.sharding import PartitionSpec as P

EXP_WIN = 2
QUAD = 4
PAD = 16
CHUNKS = 2
DOWN_STEPS = 4
RELAY = (2, 1)
RELAY_BACK = (1, 2)
MESH = pl.DeviceIdType.MESH
F32 = jnp.float32
BF16 = jnp.bfloat16
NT = (((1,), (1,)), ((), ()))
TN = (((0,), (0,)), ((), ()))


def pass_kernel(
    cap,
    og_hbm,
    rw_hbm,
    rt_hbm,
    sl_hbm,
    ct_hbm,
    sgate_ref,
    sup_ref,
    gw_ref,
    uw_ref,
    dw_ref,
    tok_ref,
    hid_out,
    rows_out,
    og_ref,
    rw_ref,
    rt_ref,
    sl_ref,
    ct_ref,
    in_sem,
    gw,
    uw,
    dw,
    sg,
    su,
    rows,
    far_out,
    up,
    fac_g,
    fac_u,
    hid,
    part,
    core_out,
    core_in,
    summed,
    quad_in,
    relayed,
    far_ret,
    far_in,
    near_ret,
    w_sem,
    l_sem,
    o_sem,
    sv_send,
    sv_recv,
    fd_send,
    fd_recv,
    qd_send,
    qd_recv,
    cd_send,
    cd_recv,
    cr_send,
    cr_recv,
    qr_send,
    qr_recv,
    fr_send,
    fr_recv,
):
    g = lax.axis_index("groups")
    e = lax.axis_index("expert")
    d = lax.axis_index("dp")
    half = e // QUAD
    r = e % QUAD
    far = (1 - half) * QUAD + r
    core_peer = (g, e, 1 - d)
    far_peer = (g, far, d)

    def quad_rank(rel):
        hi, lo = r // 2, r % 2
        if rel & 2:
            hi = 1 - hi
        if rel & 1:
            lo = 1 - lo
        return hi * 2 + lo

    def quad_peer(rel):
        return (g, half * QUAD + quad_rank(rel), d)

    ff = dw.shape[0]
    width = dw.shape[1]
    step = width // CHUNKS
    group = rows.shape[0] // 2

    small = [
        pltpu.make_async_copy(src, dst, in_sem.at[i])
        for i, (src, dst) in enumerate(
            (
                (rt_hbm, rt_ref),
                (sl_hbm, sl_ref),
                (ct_hbm, ct_ref),
                (rw_hbm, rw_ref),
                (og_hbm, og_ref),
            )
        )
    ]
    for c in small:
        c.start()
    mine = pl.multiple_of(d * ff, ff)
    loads = [
        pltpu.make_async_copy(sgate_ref.at[0, :, pl.ds(mine, ff)], sg.at[d], l_sem.at[0]),
        pltpu.make_async_copy(sup_ref.at[0, :, pl.ds(mine, ff)], su.at[d], l_sem.at[1]),
    ]
    for c in loads:
        c.start()
    w_dw = [
        pltpu.make_async_copy(
            dw_ref.at[pl.ds(mine, ff), pl.ds(c * step, step)],
            dw.at[:, pl.ds(c * step, step)],
            w_sem.at[0, c],
        )
        for c in range(CHUNKS)
    ]
    w_gw = [
        pltpu.make_async_copy(
            gw_ref.at[pl.ds(c * step, step), pl.ds(mine, ff)],
            gw.at[pl.ds(c * step, step), :],
            w_sem.at[1, c],
        )
        for c in range(CHUNKS)
    ]
    w_uw = [
        pltpu.make_async_copy(
            uw_ref.at[pl.ds(c * step, step), pl.ds(mine, ff)],
            uw.at[pl.ds(c * step, step), :],
            w_sem.at[2, c],
        )
        for c in range(CHUNKS)
    ]
    barrier = pltpu.get_barrier_semaphore()
    for peer in (core_peer, far_peer, quad_peer(1), quad_peer(2)):
        pl.semaphore_signal(barrier, inc=1, device_id=peer, device_id_type=MESH)
    pl.semaphore_wait(barrier, 4)

    def remote(src, dst, ss, rs, peer):
        return pltpu.make_async_remote_copy(
            src_ref=src, dst_ref=dst, send_sem=ss, recv_sem=rs, device_id=peer, device_id_type=MESH
        )

    theirs = pl.multiple_of((1 - d) * ff, ff)
    saved = [
        remote(
            sgate_ref.at[0, :, pl.ds(theirs, ff)], sg.at[d], sv_send.at[0], sv_recv.at[0], core_peer
        ),
        remote(
            sup_ref.at[0, :, pl.ds(theirs, ff)], su.at[d], sv_send.at[1], sv_recv.at[1], core_peer
        ),
    ]

    for c in small:
        c.wait()
    tokens = og_ref.shape[0]
    line = lax.broadcasted_iota(jnp.int32, (EXP_WIN * PAD, tokens), 0)
    line_x = line // PAD
    line_c = line % PAD
    live_count = jnp.where(line_x == 0, ct_ref[0:1, 0:1], ct_ref[0:1, 1:2])
    match = [
        (rt_ref[k : k + 1, :] == line_x) & (sl_ref[k : k + 1, :] == line_c) & (line_c < cap)
        for k in range(2)
    ]
    placing = [
        jnp.where(m & (line_c < live_count), 1.0, 0.0).astype(BF16) for m in match
    ]
    same = lax.broadcasted_iota(jnp.int32, (tokens, tokens), 0) == lax.broadcasted_iota(
        jnp.int32, (tokens, tokens), 1
    )
    weight = [
        jnp.sum(jnp.where(same, rw_ref[k : k + 1, :], 0.0), axis=1, keepdims=True)
        for k in range(2)
    ]

    def slot(owner):
        return pl.multiple_of(d * group + ((owner % QUAD) * 2 + owner // QUAD) * PAD, PAD)

    def quad_copy(at, kind, source, c, rel):
        place = rows.at[pl.ds(at, PAD), pl.ds(c * step, step)]
        cp = remote(
            place, place, qd_send.at[kind, source, c], qd_recv.at[kind, source, c], quad_peer(rel)
        )
        cp.start()
        return cp

    own_at = slot(e)
    far_at = slot(far)
    far_send, quad_near, quad_far, core_send = [], [], [], []
    relay_near, relay_far = [], []
    for c in range(CHUNKS):
        cols = pl.ds(c * step, step)
        og = og_ref[:, cols].astype(F32)
        packed = jnp.zeros((EXP_WIN * PAD, step), F32)
        for k in range(2):
            scaled = (weight[k] * og).astype(BF16)
            packed = packed + jnp.dot(placing[k], scaled, preferred_element_type=F32)
        first, second = packed[:PAD], packed[PAD:]
        rows[pl.ds(own_at, PAD), cols] = jnp.where(half == 0, first, second).astype(BF16)
        far_out[:, cols] = jnp.where(half == 0, second, first).astype(BF16)
        cp = remote(
            far_out.at[:, cols],
            rows.at[pl.ds(own_at, PAD), cols],
            fd_send.at[c],
            fd_recv.at[c],
            far_peer,
        )
        cp.start()
        far_send.append(cp)
        quad_near.append([quad_copy(own_at, 0, rel - 1, c, rel) for rel in (1, 2)])
    for cp in saved:
        cp.start()
    for c in range(CHUNKS):
        w_dw[c].start()

    for cp in loads:
        cp.wait()
    for cp in saved:
        cp.wait_recv()
    samples = sg.shape[1]
    ri = lax.broadcasted_iota(jnp.int32, (group, samples), 0)
    ci = lax.broadcasted_iota(jnp.int32, (group, samples), 1)
    block = ri // PAD
    place = ri % PAD
    owner = (block % 2) * QUAD + block // 2
    spread = jnp.where((ci == owner * cap + place) & (place < cap), 1.0, 0.0).astype(BF16)
    piece = 256

    def relay(c, sent, kind):
        via = RELAY[c]
        sent[c][via - 1].wait_recv()
        source = (half if kind == 0 else 1 - half) * QUAD + quad_rank(via)
        return quad_copy(slot(source), kind, 2, c, 3 - via)

    for dd in range(2):
        for q in range(ff // piece):
            cols = pl.ds(q * piece, piece)
            at = pl.ds(dd * group, group)
            gv = jnp.dot(spread, sg[dd, :, cols], preferred_element_type=F32)
            uv = jnp.dot(spread, su[dd, :, cols], preferred_element_type=F32)
            s = jax.nn.sigmoid(gv)
            gs = gv * s
            fac_u[at, cols] = gs
            fac_g[at, cols] = uv * s * (1.0 + gv * (1.0 - s))
            hid[cols, at] = jnp.transpose(gs * uv).astype(BF16)
            if dd == 1 and q < CHUNKS:
                relay_near.append(relay(q, quad_near, 0))
    out_hid = pltpu.make_async_copy(hid, hid_out, o_sem.at[0])
    out_hid.start()

    own_rows = pl.ds(pl.multiple_of(d * group, group), group)
    other_rows = pl.ds(pl.multiple_of((1 - d) * group, group), group)

    def upstream_chunk(c):
        cols = pl.ds(c * step, step)
        core_send[c].wait_recv()
        w_dw[c].wait()
        term = lax.dot_general(rows[:, cols], dw[:, cols], NT, preferred_element_type=F32)
        if c == 0:
            up[...] = term
        else:
            up[...] += term

    for t in range(CHUNKS + 3):
        if t < CHUNKS:
            far_send[t].wait_recv()
            quad_far.append([quad_copy(far_at, 1, rel - 1, t, rel) for rel in (1, 2)])
            w_gw[t].start()
            w_uw[t].start()
        if 0 <= t - 1 < CHUNKS:
            relay_far.append(relay(t - 1, quad_far, 1))
        if 0 <= t - 2 < CHUNKS:
            c = t - 2
            cols = pl.ds(c * step, step)
            straight = 2 - RELAY[c]
            quad_near[c][straight].wait_recv()
            quad_far[c][straight].wait_recv()
            relay_near[c].wait_recv()
            relay_far[c].wait_recv()
            cp = remote(
                rows.at[own_rows, cols],
                rows.at[own_rows, cols],
                cd_send.at[c],
                cd_recv.at[c],
                core_peer,
            )
            cp.start()
            core_send.append(cp)
        if t >= 3:
            upstream_chunk(t - 3)
    out_rows = pltpu.make_async_copy(rows, rows_out, o_sem.at[1])
    out_rows.start()

    gg = (up[...] * fac_g[...]).astype(BF16)
    gu = (up[...] * fac_u[...]).astype(BF16)

    core_ret, quad_ret, far_back = [], [], []

    sub = step // 2

    def stage_first(c):
        w_gw[c].wait()
        w_uw[c].wait()
        returned_piece(c, 0)

    def returned_piece(c, piece):
        at = pl.ds(c * step + piece * sub, sub)
        part[c, :, pl.ds(piece * sub, sub)] = lax.dot_general(
            gg, gw[at, :], NT, preferred_element_type=F32
        ) + lax.dot_general(gu, uw[at, :], NT, preferred_element_type=F32)

    def stage_a(c):
        returned_piece(c, 1)
        core_out[c] = part[c, other_rows, :].astype(BF16)
        cp = remote(core_out.at[c], core_in.at[c], cr_send.at[c], cr_recv.at[c], core_peer)
        cp.start()
        core_ret.append(cp)

    def stage_b(c):
        core_ret[c].wait_recv()
        summed[c] = (part[c, own_rows, :] + core_in[c].astype(F32)).astype(BF16)
        via = RELAY_BACK[c]
        copies = []
        for i, rank in enumerate((quad_rank(via), quad_rank(3))):
            cp = remote(
                summed.at[c, pl.ds(pl.multiple_of(rank * 2 * PAD, 2 * PAD), 2 * PAD), :],
                quad_in.at[i, c],
                qr_send.at[i, c],
                qr_recv.at[i, c],
                quad_peer(via),
            )
            cp.start()
            copies.append(cp)
        quad_ret.append(copies)

    def stage_r(c):
        rel = 3 - RELAY_BACK[c]
        quad_ret[c][1].wait_recv()
        at = pl.multiple_of(quad_rank(rel) * 2 * PAD, 2 * PAD)
        relayed[c] = (
            summed[c, pl.ds(at, 2 * PAD), :].astype(F32) + quad_in[1, c].astype(F32)
        ).astype(BF16)
        cp = remote(
            relayed.at[c], quad_in.at[2, c], qr_send.at[2, c], qr_recv.at[2, c], quad_peer(rel)
        )
        cp.start()
        quad_ret[c].append(cp)

    def stage_c(c):
        quad_ret[c][0].wait_recv()
        quad_ret[c][2].wait_recv()
        at = pl.multiple_of(r * 2 * PAD, 2 * PAD)
        total = summed[c, pl.ds(at, 2 * PAD), :].astype(F32)
        total = total + quad_in[0, c].astype(F32) + quad_in[2, c].astype(F32)
        first, second = total[:PAD], total[PAD:]
        near_ret[c] = jnp.where(half == 0, first, second)
        far_ret[c] = jnp.where(half == 0, second, first).astype(BF16)
        cp = remote(far_ret.at[c], far_in.at[c], fr_send.at[c], fr_recv.at[c], far_peer)
        cp.start()
        far_back.append(cp)

    table = jnp.where(match[0], 1.0, 0.0) + jnp.where(match[1], 1.0, 0.0)
    table_near = jnp.where(half == 0, table[:PAD], table[PAD:]).astype(BF16)
    table_far = jnp.where(half == 0, table[PAD:], table[:PAD]).astype(BF16)

    def stage_d(c):
        far_back[c].wait_recv()
        near = near_ret[c]
        high = near.astype(BF16)
        low = (near - high.astype(F32)).astype(BF16)
        total = lax.dot_general(table_near, high, TN, preferred_element_type=F32)
        total = total + lax.dot_general(table_near, low, TN, preferred_element_type=F32)
        total = total + lax.dot_general(table_far, far_in[c], TN, preferred_element_type=F32)
        tok_ref[:, pl.ds(c * step, step)] = total.astype(BF16)

    for t in range(CHUNKS + 4):
        order = (stage_first, stage_b, stage_a, stage_r, stage_c, stage_d)
        for lag, stage in zip((0, 1, 0, 2, 3, 4), order):
            if 0 <= t - lag < CHUNKS:
                stage(t - lag)

    out_hid.wait()
    out_rows.wait()
    for cp in saved + far_send + relay_near + relay_far + core_send + core_ret + far_back:
        cp.wait_send()
    for group_of in quad_near + quad_far + quad_ret:
        for cp in group_of:
            cp.wait_send()


def down_kernel(hid_ref, rows_ref, out_ref):
    out_ref[...] = jnp.dot(hid_ref[...], rows_ref[...], preferred_element_type=F32)


def local_fast(og, rw, rt, sl, ct, sgate, sup, gw, uw, dw):
    tokens, width = og.shape
    ff = dw.shape[0] // 2
    samples = sgate.shape[1]
    owners = lax.axis_size("expert")
    cap = samples // owners
    group = owners * PAD
    step = width // CHUNKS
    vmem = pl.BlockSpec(memory_space=pltpu.VMEM)
    hbm = pl.BlockSpec(memory_space=pl.ANY)
    dma = pltpu.SemaphoreType.DMA
    tok, hid, rows = pl.pallas_call(
        functools.partial(pass_kernel, cap),
        out_shape=(
            jax.ShapeDtypeStruct((tokens, width), BF16),
            jax.ShapeDtypeStruct((ff, 2 * group), BF16),
            jax.ShapeDtypeStruct((2 * group, width), BF16),
        ),
        in_specs=[hbm] * 10,
        out_specs=(vmem, hbm, hbm),
        scratch_shapes=[
            pltpu.VMEM(og.shape, BF16),
            pltpu.VMEM((2, tokens), F32),
            pltpu.VMEM((2, tokens), jnp.int32),
            pltpu.VMEM((2, tokens), jnp.int32),
            pltpu.VMEM(ct.shape, jnp.int32),
            dma((5,)),
            pltpu.VMEM((width, ff), BF16),
            pltpu.VMEM((width, ff), BF16),
            pltpu.VMEM((ff, width), BF16),
            pltpu.VMEM((2, samples, ff), BF16),
            pltpu.VMEM((2, samples, ff), BF16),
            pltpu.VMEM((2 * group, width), BF16),
            pltpu.VMEM((PAD, width), BF16),
            pltpu.VMEM((2 * group, ff), F32),
            pltpu.VMEM((2 * group, ff), F32),
            pltpu.VMEM((2 * group, ff), F32),
            pltpu.VMEM((ff, 2 * group), BF16),
            pltpu.VMEM((CHUNKS, 2 * group, step), F32),
            pltpu.VMEM((CHUNKS, group, step), BF16),
            pltpu.VMEM((CHUNKS, group, step), BF16),
            pltpu.VMEM((CHUNKS, group, step), BF16),
            pltpu.VMEM((3, CHUNKS, 2 * PAD, step), BF16),
            pltpu.VMEM((CHUNKS, 2 * PAD, step), BF16),
            pltpu.VMEM((CHUNKS, PAD, step), BF16),
            pltpu.VMEM((CHUNKS, PAD, step), BF16),
            pltpu.VMEM((CHUNKS, PAD, step), F32),
            dma((3, CHUNKS)),
            dma((2,)),
            dma((2,)),
            dma((2,)),
            dma((2,)),
            dma((CHUNKS,)),
            dma((CHUNKS,)),
            dma((2, 3, CHUNKS)),
            dma((2, 3, CHUNKS)),
            dma((CHUNKS,)),
            dma((CHUNKS,)),
            dma((CHUNKS,)),
            dma((CHUNKS,)),
            dma((3, CHUNKS)),
            dma((3, CHUNKS)),
            dma((CHUNKS,)),
            dma((CHUNKS,)),
        ],
        compiler_params=pltpu.CompilerParams(
            collective_id=0, has_side_effects=True, vmem_limit_bytes=60 * 1024 * 1024
        ),
        cost_estimate=pl.CostEstimate(
            flops=12 * group * ff * width, bytes_accessed=6 * ff * width, transcendentals=2 * group * ff
        ),
    )(og, rw.T, rt.T, sl.T, ct, sgate, sup, gw, uw, dw)
    tile = width // DOWN_STEPS
    down = pl.pallas_call(
        down_kernel,
        grid=(DOWN_STEPS,),
        in_specs=[
            pl.BlockSpec((ff, 2 * group), lambda i: (0, 0)),
            pl.BlockSpec((2 * group, tile), lambda i: (0, i)),
        ],
        out_specs=pl.BlockSpec((ff, tile), lambda i: (0, i)),
        out_shape=jax.ShapeDtypeStruct((ff, width), F32),
        compiler_params=pltpu.CompilerParams(vmem_limit_bytes=62 * 1024 * 1024),
        cost_estimate=pl.CostEstimate(
            flops=4 * group * ff * width, bytes_accessed=4 * ff * width, transcendentals=0
        ),
    )(hid, rows)
    return tok, down


def local_plain(og, rw, rt, sl, ct, sgate, sup, gw, uw, dw):
    senders = lax.axis_size("expert")
    shards = senders // EXP_WIN
    capacity = sgate.shape[1] // senders
    tokens, width = og.shape
    places = jnp.arange(capacity, dtype=jnp.int32)
    experts = jnp.arange(EXP_WIN, dtype=jnp.int32)
    matches = (rt[:, :, None, None] == experts[None, None, :, None]) & (
        sl[:, :, None, None] == places[None, None, None, :]
    )
    live = places[None, :] < ct[0][:, None]
    scaled = (rw[:, :, None] * og[:, None, :].astype(F32)).astype(BF16)
    placing = (matches & live[None, None, :, :]).astype(BF16)
    packed = jnp.einsum("tkxc,tkd->xcd", placing, scaled, preferred_element_type=F32).astype(BF16)
    outgoing = jnp.repeat(packed, shards, axis=0)
    arrived = lax.all_to_all(outgoing, "expert", split_axis=0, concat_axis=0, tiled=True)
    rows = arrived.reshape(senders * capacity, width)
    gv = sgate[0].astype(F32)
    uv = sup[0].astype(F32)
    upstream = lax.dot_general(rows, dw, NT, preferred_element_type=F32)
    s = jax.nn.sigmoid(gv)
    grad_up = (upstream * gv * s).astype(BF16)
    grad_gate = (upstream * uv * s * (1.0 + gv * (1.0 - s))).astype(BF16)
    hidden = (gv * s * uv).astype(BF16)
    part = lax.dot_general(grad_gate, gw, NT, preferred_element_type=F32)
    part = part + lax.dot_general(grad_up, uw, NT, preferred_element_type=F32)
    table = jnp.sum(matches.astype(F32), axis=1).reshape(tokens, EXP_WIN * capacity)
    received = lax.all_to_all(
        part.astype(BF16).reshape(senders, capacity, width),
        "expert",
        split_axis=0,
        concat_axis=0,
        tiled=True,
    )
    summed = jnp.sum(received.reshape(EXP_WIN, shards, capacity, width), axis=1, dtype=F32)
    gathered = jnp.dot(
        table,
        summed.reshape(EXP_WIN * capacity, width),
        precision=lax.Precision.HIGHEST,
        preferred_element_type=F32,
    )
    both_hidden = lax.all_to_all(hidden, "dp", split_axis=1, concat_axis=0, tiled=True)
    both_rows = lax.all_gather(rows, "dp", axis=0, tiled=True)
    down = lax.dot_general(both_hidden, both_rows, TN, preferred_element_type=F32)
    return gathered.astype(BF16), down


def solution(mesh):
    tokens = P(("groups", "expert", "dp"), None)
    saved = P(("groups", "dp"), None, "expert")
    columns = P(None, "expert")
    fits = mesh.shape["expert"] == EXP_WIN * QUAD and mesh.shape["dp"] == 2
    return jax.shard_map(
        local_fast if fits else local_plain,
        mesh=mesh,
        in_specs=(tokens,) * 5 + (saved, saved, columns, columns, P("expert", None)),
        out_specs=(tokens, tokens),
        check_vma=False,
    )
```
